32 devices in a mesh: blk: 4 (over y, x), grp: 8 (over z, core).
Axes of the slice: x: 2, y: 2, z: 4, core: 2. Of those that a mesh axis runs over, the one named last changes fastest.
Arguments:
- centres: float32 [3, 32768], P(None, ('blk', 'grp')), may hold values from -8 to 8, as said below
- coeffs: float32 [3, 32768], P(None, ('blk', 'grp')), may hold values from -2 to 5.5
- residual: float32 [3, 32768], P(None, ('blk', 'grp')), may hold values from -18 to 18
- direction_prev: float32 [3, 32768], P(None, ('blk', 'grp')), may hold values from -6 to 6
- smoothing: float32 [32768], P(('blk', 'grp')), may hold values from 0.5 to 5
- norm_prev: float32 [3], replicated, may hold values from 32768 to 131072
- support_radius: int32 [1], replicated, may hold values from 900 to 960
- volume_nodes: float32 [3, 32768], P(None, ('blk', 'grp')), may hold values from -10 to 10
- block_lists: int32 [32, 4], P(('blk', 'grp')), may hold values from 0 to 7, as said below
Outputs:
- coeffs_next: float32 [3, 32768], P(None, ('blk', 'grp'))
- residual_next: float32 [3, 32768], P(None, ('blk', 'grp'))
- direction: float32 [3, 32768], P(None, ('blk', 'grp'))
- norm_next: float32 [3], replicated
- displacement: float32 [3, 32768], P(None, ('blk', 'grp'))
The draws below stay inside these ranges and needn't reach their ends.
Inputs may be any that keep to these rules, and one draw needn't show every extreme that they name: `centres`: every centre of block k has its distance from the z axis within [g, g + 1) with g = k mod 8, and lies at height -0.01 times the square of that distance. `block_lists`: each row names 4 different bands.
All inputs are finite; a program needn't handle non-finite values.
Results may differ from the reference program's by a relative error of at most 0.0003.
Values sent between devices are 32-bit elements; how exact they have to be, the bound alone decides.
A program may use at most 64 MiB of HBM per device.

```python
import math
import jax
import jax.numpy as jnp
from jax import lax

C_DEV = 1024
V_DEV = 1024
LIST = 4
NC = 32768
N_BLK = 4
N_GRP = 8


CURVE = 0.01


def band_lists(key):
    inner = jax.random.fold_in(key, 17)
    total = N_BLK * N_GRP
    scores = jax.random.randint(inner, (total, N_GRP), 0, 1 << 20) * N_GRP + jnp.arange(N_GRP, dtype=jnp.int32)[None, :]
    order = jnp.argsort(scores, axis=1)
    return order[:, :LIST].astype(jnp.int32)


def draw_block_lists(key, part):
    return band_lists(key)


def draw_volume_nodes(key, part):
    lists = band_lists(key)
    total = N_BLK * N_GRP
    inner = jax.random.fold_in(key, 29)
    first, second, third = jax.random.split(inner, 3)
    slot = jnp.arange(V_DEV) % LIST
    bands = lists[:, slot].astype(jnp.float32)
    sector = (jnp.arange(total) // N_GRP).astype(jnp.float32)[:, None]
    turn = jax.random.uniform(first, (total, V_DEV), jnp.float32)
    angle = 2.0 * math.pi * (sector + turn) / N_BLK
    offset = jax.random.uniform(second, (total, V_DEV), jnp.float32, -0.5, 1.5)
    distance = jnp.maximum(bands + offset, 0.0)
    lift = jax.random.uniform(third, (total, V_DEV), jnp.float32, 0.8, 0.9)
    stacked = jnp.stack([distance * jnp.cos(angle), distance * jnp.sin(angle), lift - CURVE * distance * distance])
    return stacked.reshape(3, total * V_DEV)


def draw_centres(key, part):
    total = N_BLK * N_GRP
    inner = jax.random.fold_in(key, 41)
    first, second = jax.random.split(inner, 2)
    sector = (jnp.arange(total) // N_GRP).astype(jnp.float32)[:, None]
    band = (jnp.arange(total) % N_GRP).astype(jnp.float32)[:, None]
    turn = jax.random.uniform(first, (total, C_DEV), jnp.float32)
    radial = jax.random.uniform(second, (total, C_DEV), jnp.float32)
    angle = 2.0 * math.pi * (sector + turn) / N_BLK
    distance = band + radial
    stacked = jnp.stack([distance * jnp.cos(angle), distance * jnp.sin(angle), -CURVE * distance * distance])
    return stacked.reshape(3, total * C_DEV)


def draw_coeffs(key, part):
    total = N_BLK * N_GRP
    inner = jax.random.fold_in(key, 67)
    values = 1.5 + 0.8 * jnp.clip(jax.random.normal(inner, (3, total * C_DEV), jnp.float32), -4.0, 4.0)
    return values


def draw_residual(key, part):
    total = N_BLK * N_GRP
    inner = jax.random.fold_in(key, 53)
    rising = jnp.exp(math.log(3.0) * jnp.arange(total, dtype=jnp.float32) / (total - 1))
    base = jnp.clip(jax.random.normal(inner, (3, total, C_DEV), jnp.float32), -6.0, 6.0)
    return (base * rising[None, :, None]).reshape(3, total * C_DEV)


def block_levels(rng, shape, pieces, smallest, high):
    loudness = 1.0
    for axis_at, parts in pieces:
        draws = jax.random.uniform(jax.random.fold_in(jax.random.fold_in(rng, 6), axis_at), (parts,), jnp.float32, smallest / len(pieces), high / len(pieces))
        loudness = loudness * jnp.repeat(jnp.exp(draws), shape[axis_at] // parts).reshape((-1,) + (1,) * (len(shape) - 1 - axis_at))
    return loudness


def noise(stream_key, shape, scale, most, cuts=(), kind=jnp.bfloat16):
    factor_of = block_levels(stream_key, shape, cuts, -0.22, 0.18) if cuts else 1.0
    array = jax.random.normal(stream_key, shape, jnp.float32) * scale * factor_of
    return jnp.minimum(jnp.maximum(array, -most), most).astype(kind)


def setup_inputs(seed: int = 0) -> dict:
    keys = jax.random.split(jax.random.key(seed), 10)
    centres = draw_centres(jax.random.fold_in(keys[9], 71), 0)
    coeffs = draw_coeffs(jax.random.fold_in(keys[9], 71), 0)
    residual = draw_residual(jax.random.fold_in(keys[9], 71), 0)
    direction_prev = noise(keys[3], (3, NC), 1.0, 6.0, ((1, 32),), jnp.float32)
    smoothing = jnp.clip(jnp.exp(math.log(5.0) - 2.3025851 * jax.random.uniform(keys[4], (NC,), jnp.float32) ** block_levels(keys[4], (NC,), ((0, 32),), -0.2, 0.2)), 0.5, 5.0)
    norm_prev = jnp.clip(jnp.exp(jax.random.uniform(keys[5], (3,), jnp.float32, math.log(32768.0), math.log(131072.0))), 32768.0, 131072.0)
    support_radius = jax.random.randint(keys[6], (1,), 900, 961).astype(jnp.int32)
    volume_nodes = draw_volume_nodes(jax.random.fold_in(keys[9], 71), 0)
    block_lists = draw_block_lists(jax.random.fold_in(keys[9], 71), 0)
    return {"centres": centres, "coeffs": coeffs, "residual": residual, "direction_prev": direction_prev, "smoothing": smoothing, "norm_prev": norm_prev, "support_radius": support_radius, "volume_nodes": volume_nodes, "block_lists": block_lists}


RADIUS_UNIT = 0.001

def wendland(sources, targets, radius):
    apart_first = sources[0][:, None] - targets[0][None, :]
    apart_second = sources[1][:, None] - targets[1][None, :]
    apart_third = sources[2][:, None] - targets[2][None, :]
    distance = jnp.sqrt(apart_first * apart_first + apart_second * apart_second + apart_third * apart_third)
    scaled = distance / radius
    remain = jnp.maximum(1.0 - scaled, 0.0)
    square = remain * remain
    return square * square * (4.0 * scaled + 1.0)

def kernel_product(centres, direction, radius):
    total = N_BLK * N_GRP
    count = centres.shape[1] // total
    zero = jnp.zeros((), jnp.int32)
    places = centres.reshape(3, N_BLK, N_GRP, count)
    values = direction.reshape(3, N_BLK, N_GRP, count)
    padding = jnp.zeros((3, N_BLK, 1, count), jnp.float32)
    places_pad = jnp.concatenate([padding, places, padding], axis=2)
    values_pad = jnp.concatenate([padding, values, padding], axis=2)

    def one_block(index):
        sector = index // N_GRP
        band = index % N_GRP
        targets = lax.dynamic_slice(places, (zero, sector, band, zero), (3, 1, 1, count)).reshape(3, count)
        near_places = lax.dynamic_slice(places_pad, (zero, zero, band, zero), (3, N_BLK, 3, count)).reshape(3, N_BLK * 3 * count)
        near_values = lax.dynamic_slice(values_pad, (zero, zero, band, zero), (3, N_BLK, 3, count)).reshape(3, N_BLK * 3 * count)
        weights = wendland(near_places, targets, radius)
        return jnp.dot(near_values, weights, preferred_element_type=jnp.float32, precision=lax.Precision.HIGHEST)
    result = lax.map(one_block, jnp.arange(total, dtype=jnp.int32))
    return result.transpose(1, 0, 2).reshape(3, total * count)

def evaluate(centres, coeffs_next, volume_nodes, block_lists, radius):
    total = N_BLK * N_GRP
    count = centres.shape[1] // total
    per_block = volume_nodes.shape[1] // total
    zero = jnp.zeros((), jnp.int32)
    places = centres.reshape(3, N_BLK, N_GRP, count)
    values = coeffs_next.reshape(3, N_BLK, N_GRP, count)
    nodes = volume_nodes.reshape(3, total, per_block)

    def one_block(index):
        sector = index // N_GRP
        targets = lax.dynamic_slice(nodes, (zero, index, zero), (3, 1, per_block)).reshape(3, per_block)
        listed = block_lists[index]

        def one_entry(carry, band):
            band = band.astype(jnp.int32)
            sources = lax.dynamic_slice(places, (zero, sector, band, zero), (3, 1, 1, count)).reshape(3, count)
            weights_in = lax.dynamic_slice(values, (zero, sector, band, zero), (3, 1, 1, count)).reshape(3, count)
            weights = wendland(sources, targets, radius)
            return (carry + jnp.dot(weights_in, weights, preferred_element_type=jnp.float32, precision=lax.Precision.HIGHEST), None)
        result, _ = lax.scan(one_entry, jnp.zeros((3, per_block), jnp.float32), listed)
        return result
    result = lax.map(one_block, jnp.arange(total, dtype=jnp.int32))
    return result.transpose(1, 0, 2).reshape(3, total * per_block)

def reference(centres, coeffs, residual, direction_prev, smoothing, norm_prev, support_radius, volume_nodes, block_lists):
    radius = support_radius[0].astype(jnp.float32) * RADIUS_UNIT
    scaling = 1.0 + smoothing
    precond = residual / scaling
    norm_now = lax.optimization_barrier(jnp.sum(residual * precond, axis=1))
    beta = norm_now / norm_prev
    direction = precond + beta[:, None] * direction_prev
    image = smoothing * direction + kernel_product(centres, direction, radius)
    curvature = lax.optimization_barrier(jnp.sum(direction * image, axis=1))
    alpha = norm_now / curvature
    coeffs_next = coeffs + alpha[:, None] * direction
    residual_next = residual - alpha[:, None] * image
    norm_next = lax.optimization_barrier(jnp.sum(residual_next * residual_next / scaling, axis=1))
    displacement = evaluate(centres, coeffs_next, volume_nodes, block_lists, radius)
    return (coeffs_next, residual_next, direction, norm_next, displacement)
```

```python
import functools
import jax
import jax.numpy as jnp
from jax import lax
from jax.experimental import pallas as pl
from jax.experimental.pallas import tpu as pltpu
from jax.sharding import PartitionSpec as P

RADIUS_UNIT = 0.001
CURVE = 0.01
F32 = jnp.float32
BF16 = jnp.bfloat16
MESH = pl.DeviceIdType.MESH


def rounded(value):
    return value.astype(BF16).astype(F32)


def pieces(coords):
    high = jnp.floor(coords * 4.0 + 0.5) * 0.25
    rest = coords - high
    low = rounded(rest)
    lower = rounded(rest - low)
    big = jnp.sum(high * high, axis=0, keepdims=True)
    small = jnp.sum(rest * (2.0 * high + rest), axis=0, keepdims=True)
    big_a = rounded(big)
    small_a = rounded(small)
    small_b = rounded(small - small_a)
    return high, low, lower, (big_a, big - big_a), (small_a, small_b, small - small_a - small_b)


def rows_of(base, row, first, values):
    for index, value in enumerate(values):
        base = jnp.where(row == first + index, value, base)
    return base


def source_factor(coords, row):
    high, low, lower, big, small = pieces(coords)
    one = 1.0
    return jnp.concatenate(
        [
            rows_of(high, row, 3, big + (one, one)),
            rows_of(low, row, 3, small),
            rows_of(lower, row, 3, (one, one, one)),
            high,
            high,
            low,
            lower,
            low,
        ],
        axis=0,
    ).astype(BF16)


def target_factor(coords, row):
    high, low, lower, big, small = pieces(coords)
    high, low, lower = -2.0 * high, -2.0 * low, -2.0 * lower
    one = 1.0
    return jnp.concatenate(
        [
            rows_of(high, row, 3, (one, one) + big),
            rows_of(high, row, 3, (one, one, one)),
            rows_of(high, row, 3, small),
            low,
            lower,
            low,
            low,
            lower,
        ],
        axis=0,
    )


def kernel(
    blk,
    grp,
    centres,
    coeffs,
    residual,
    direction_prev,
    smoothing,
    norm_prev,
    support_radius,
    nodes,
    lists,
    coeffs_next,
    residual_next,
    direction_out,
    norm_next,
    displacement,
    slots,
    coeff_slots,
    factor_c,
    factor_v,
    factor_s,
    values,
    acc,
    acc_v,
    red_blk,
    red_grp,
    send_sem,
    recv_sem,
    csend_sem,
    crecv_sem,
    bsend_sem,
    brecv_sem,
    gsend_sem,
    grecv_sem,
):
    s = lax.axis_index("blk")
    g = lax.axis_index("grp")
    count = centres.shape[1]
    near = 3 * blk
    tile = 256

    def plan(i):
        k = i % blk
        j = i // blk
        return k, j, jnp.where(j == 1, -1, jnp.where(j == 2, 1, 0))

    def near_copy(i, start):
        k, j, shift = plan(i)
        to_s = lax.rem(s - k + blk, blk)
        to_g = g - shift
        slot = jnp.where(k == 0, g, grp + (k - 1) * 3 + j)

        @pl.when((to_g >= 0) & (to_g < grp))
        def _():
            start(to_s, to_g, slot, i)

    def far_loop(start):
        def step(m, _):
            to_g = lax.rem(g + m, grp)

            @pl.when((to_g - g > 1) | (g - to_g > 1))
            def _():
                start(s, to_g, g, near + m)

            return 0

        lax.fori_loop(1, grp, step, 0)

    def copy_of(to_s, to_g, slot, sem):
        return pltpu.make_async_remote_copy(
            src_ref=slots.at[g],
            dst_ref=slots.at[slot],
            send_sem=send_sem.at[sem],
            recv_sem=recv_sem.at[slot],
            device_id=(to_s, to_g),
            device_id_type=MESH,
        )

    def coeff_copy(m, slot):
        return pltpu.make_async_remote_copy(
            src_ref=coeff_slots.at[g],
            dst_ref=coeff_slots.at[slot],
            send_sem=csend_sem.at[m],
            recv_sem=crecv_sem.at[slot],
            device_id=(s, lax.rem(g + m, grp)),
            device_id_type=MESH,
        )

    barrier = pltpu.get_barrier_semaphore()

    def greet(to_s, to_g, slot, sem):
        pl.semaphore_signal(barrier, inc=1, device_id=(to_s, to_g), device_id_type=MESH)

    def near_loop(start):
        def step(i, _):
            near_copy(i, start)
            return 0

        lax.fori_loop(1, near, step, 0)

    near_loop(greet)
    far_loop(greet)

    weight = 1.0 / (1.0 + smoothing[...])
    precond = residual[...] * weight
    slots[g] = jnp.concatenate(
        [precond, direction_prev[...], centres[0:2, :]], axis=0
    )
    coeff_slots[g] = jnp.concatenate([coeffs[...], jnp.zeros((1, count), F32)], axis=0)

    bands = 3 - jnp.where(g == 0, 1, 0) - jnp.where(g == grp - 1, 1, 0)
    pl.semaphore_wait(barrier, grp - 1 + (blk - 1) * bands)

    near_loop(lambda to_s, to_g, slot, sem: copy_of(to_s, to_g, slot, sem).start())
    far_loop(lambda to_s, to_g, slot, sem: copy_of(to_s, to_g, slot, sem).start())

    def start_coeffs(m, _):
        coeff_copy(m, g).start()
        return 0

    lax.fori_loop(1, grp, start_coeffs, 0)

    radius = support_radius[0].astype(F32) * RADIUS_UNIT
    row = lax.broadcasted_iota(jnp.int32, (8, count), 0)
    gap = jnp.zeros((5, count), F32)
    factor_c[...] = target_factor(jnp.concatenate([centres[...], gap], axis=0), row).T.astype(BF16)
    factor_v[...] = target_factor(jnp.concatenate([nodes[...], gap], axis=0), row).T.astype(BF16)
    acc[...] = jnp.zeros_like(acc)
    acc_v[...] = jnp.zeros_like(acc_v)

    def prepare(block, coeff):
        first = block[6:7, :]
        second = block[7:8, :]
        third = (first * first + second * second) * (-CURVE)
        coords = rows_of(jnp.zeros((8, count), F32), row, 0, (first, second, third))
        factor_s[...] = source_factor(coords, row)
        high = rounded(block)
        parts = [high, block - high]
        if coeff is not None:
            chigh = rounded(coeff)
            parts += [chigh, coeff - chigh, jnp.zeros((8, count), F32)]
        values[0 : 32 if coeff is not None else 16, :] = jnp.concatenate(parts, axis=0).astype(BF16)

    def product(factor, total, rows):
        def step(at, _):
            start = pl.multiple_of(at * tile, tile)
            left = factor[pl.ds(start, tile), :]
            out = jnp.zeros((tile, rows), F32)
            for cut in range(0, count, tile):
                apart = jnp.dot(
                    left, factor_s[:, cut : cut + tile], preferred_element_type=F32
                )
                apart = jnp.maximum(apart, 1e-12)
                remain = jnp.maximum(radius - apart * lax.rsqrt(apart), 0.0)
                square = remain * remain
                weights = square * square * (1.25 * radius - remain)
                whole = weights.astype(BF16)
                part = (weights - whole.astype(F32)).astype(BF16)
                right = values[0:rows, cut : cut + tile]
                contract = (((1,), (1,)), ((), ()))
                out += lax.dot_general(whole, right, contract, preferred_element_type=F32)
                out += lax.dot_general(part, right, contract, preferred_element_type=F32)
            total[pl.ds(start, tile), 0:rows] += out
            return 0

        lax.fori_loop(0, count // tile, step, 0)

    def near_block(i, _):
        k, j, shift = plan(i)
        band = g + shift

        @pl.when((band >= 0) & (band < grp))
        def _():
            slot = jnp.where(k == 0, band, grp + (k - 1) * 3 + j)

            @pl.when(i > 0)
            def _():
                copy_of(s, g, slot, i).wait_recv()

            prepare(slots[slot], None)
            product(factor_c, acc, 16)

        return 0

    lax.fori_loop(0, near, near_block, 0)

    rescale = 4.0 / (radius * radius * radius * radius * radius)
    turned = acc[...].T
    applied = (turned[0:8, :] + turned[8:16, :]) * rescale
    smooth = smoothing[...]
    previous = direction_prev[...]
    image_p = smooth * precond + applied[0:3, :]
    image_d = smooth * previous + applied[3:6, :]
    lane = lax.broadcasted_iota(jnp.int32, (3, 128), 1)
    terms = (
        residual[...] * precond,
        precond * image_p,
        precond * image_d,
        previous * image_p,
        previous * image_d,
        image_p * image_p * weight,
        image_p * image_d * weight,
        image_d * image_d * weight,
    )
    packed = jnp.zeros((3, 128), F32)
    for index, term in enumerate(terms):
        packed = jnp.where(lane == index, jnp.sum(term, axis=1, keepdims=True), packed)
    filled = jnp.concatenate([packed, jnp.zeros((5, 128), F32)], axis=0)

    red_blk[s] = filled

    def blk_copy(m, slot):
        return pltpu.make_async_remote_copy(
            src_ref=red_blk.at[s],
            dst_ref=red_blk.at[slot],
            send_sem=bsend_sem.at[m],
            recv_sem=brecv_sem.at[slot],
            device_id=(lax.rem(s + m, blk), g),
            device_id_type=MESH,
        )

    for m in range(1, blk):
        blk_copy(m, s).start()

    def await_far(to_s, to_g, slot, sem):
        copy_of(s, g, to_g, sem).wait_recv()

    far_loop(await_far)

    def await_coeffs(m, _):
        coeff_copy(m, lax.rem(g + m, grp)).wait_recv()
        return 0

    lax.fori_loop(1, grp, await_coeffs, 0)

    for m in range(1, blk):
        blk_copy(m, lax.rem(s + m, blk)).wait_recv()
    red_grp[g] = jnp.sum(red_blk[...], axis=0)

    def grp_copy(m, slot):
        return pltpu.make_async_remote_copy(
            src_ref=red_grp.at[g],
            dst_ref=red_grp.at[slot],
            send_sem=gsend_sem.at[m],
            recv_sem=grecv_sem.at[slot],
            device_id=(s, lax.rem(g + m, grp)),
            device_id_type=MESH,
        )

    def start_grp(m, _):
        grp_copy(m, g).start()
        return 0

    lax.fori_loop(1, grp, start_grp, 0)

    def listed_block(entry, _):
        band = lists[0, entry]
        prepare(slots[band], coeff_slots[band])
        product(factor_v, acc_v, 32)
        return 0

    lax.fori_loop(0, lists.shape[1], listed_block, 0)

    def await_grp(m, _):
        grp_copy(m, lax.rem(g + m, grp)).wait_recv()
        return 0

    lax.fori_loop(1, grp, await_grp, 0)
    totals = jnp.sum(red_grp[...], axis=0)[0:3, :]
    now, pp, pd, dp, dd, ipp, ipd, idd = (
        jnp.sum(jnp.where(lane == index, totals, 0.0), axis=1, keepdims=True)
        for index in range(8)
    )
    beta = now / norm_prev[:, 0:1]
    curvature = pp + beta * (pd + dp) + beta * beta * dd
    alpha = now / curvature
    cross = pp + beta * pd
    square = ipp + 2.0 * beta * ipd + beta * beta * idd
    norm_next[...] = jnp.broadcast_to(
        now - 2.0 * alpha * cross + alpha * alpha * square, norm_next.shape
    )
    direction = precond + beta * previous
    direction_out[...] = direction
    coeffs_next[...] = coeffs[...] + alpha * direction
    residual_next[...] = residual[...] - alpha * (image_p + beta * image_d)
    turned_v = acc_v[...].T * rescale
    applied_v = turned_v[0:8, :] + turned_v[8:16, :]
    applied_c = turned_v[16:24, :]
    base = applied_c[0:3, :] + applied_c[4:7, :]
    displacement[...] = base + alpha * (applied_v[0:3, :] + beta * applied_v[3:6, :])

    near_loop(lambda to_s, to_g, slot, sem: copy_of(to_s, to_g, slot, sem).wait_send())
    far_loop(lambda to_s, to_g, slot, sem: copy_of(to_s, to_g, slot, sem).wait_send())

    def finish(m, _):
        coeff_copy(m, g).wait_send()
        grp_copy(m, g).wait_send()
        return 0

    lax.fori_loop(1, grp, finish, 0)
    for m in range(1, blk):
        blk_copy(m, s).wait_send()


def per_device(blk, grp, *args):
    (
        centres,
        coeffs,
        residual,
        direction_prev,
        smoothing,
        norm_prev,
        support_radius,
        nodes,
        lists,
    ) = args
    count = centres.shape[1]
    vmem = pl.BlockSpec(memory_space=pltpu.VMEM)
    smem = pl.BlockSpec(memory_space=pltpu.SMEM)
    shape = jax.ShapeDtypeStruct((3, count), F32)
    dma = pltpu.SemaphoreType.DMA
    near = 3 * blk
    slots = grp + 3 * (blk - 1)
    blocks = near + lists.shape[1]
    result = pl.pallas_call(
        functools.partial(kernel, blk, grp),
        out_shape=(
            shape,
            shape,
            shape,
            jax.ShapeDtypeStruct((3, 128), F32),
            jax.ShapeDtypeStruct((3, nodes.shape[1]), F32),
        ),
        in_specs=[vmem, vmem, vmem, vmem, vmem, vmem, smem, vmem, smem],
        out_specs=(vmem,) * 5,
        scratch_shapes=[
            pltpu.VMEM((slots, 8, count), F32),
            pltpu.VMEM((grp, 4, count), F32),
            pltpu.VMEM((count, 64), BF16),
            pltpu.VMEM((nodes.shape[1], 64), BF16),
            pltpu.VMEM((64, count), BF16),
            pltpu.VMEM((32, count), BF16),
            pltpu.VMEM((count, 128), F32),
            pltpu.VMEM((nodes.shape[1], 128), F32),
            pltpu.VMEM((blk, 8, 128), F32),
            pltpu.VMEM((grp, 8, 128), F32),
            dma((near + grp,)),
            dma((slots,)),
            dma((grp,)),
            dma((grp,)),
            dma((blk,)),
            dma((blk,)),
            dma((grp,)),
            dma((grp,)),
        ],
        compiler_params=pltpu.CompilerParams(
            collective_id=0, has_side_effects=True, vmem_limit_bytes=40 * 1024 * 1024
        ),
        cost_estimate=pl.CostEstimate(
            flops=30 * blocks * count * count,
            bytes_accessed=1 << 20,
            transcendentals=blocks * count * count,
        ),
        name="morph_step",
    )(
        centres,
        coeffs,
        residual,
        direction_prev,
        smoothing[None, :],
        jnp.broadcast_to(norm_prev[:, None], (3, 128)),
        support_radius,
        nodes,
        lists,
    )
    coeffs_next, residual_next, direction, norm_next, displacement = result
    return coeffs_next, residual_next, direction, norm_next[:, 0], displacement


def solution(mesh):
    split = P(None, ("blk", "grp"))
    placed = (
        split,
        split,
        split,
        split,
        P(("blk", "grp")),
        P(),
        P(),
        split,
        P(("blk", "grp"), None),
    )
    return jax.shard_map(
        functools.partial(per_device, mesh.shape["blk"], mesh.shape["grp"]),
        mesh=mesh,
        in_specs=placed,
        out_specs=(split, split, split, P(), split),
        check_vma=False,
    )
```
